128 devices in a mesh: group: 16 (over z, y), row: 4 (over x_lo, core), col: 2 (over x_hi).
Axes of the slice: x: 4 (x_hi: 2, x_lo: 2; x = x_hi * 2 + x_lo), y: 4, z: 4, core: 2. Of those that a mesh axis runs over, the one named last changes fastest.
Arguments:
- front_entries: bfloat16 [16, 20480, 512], P('group', 'row', 'col'), as said below
- contrib: bfloat16 [16, 4, 2, 16, 4, 8, 128, 128], P('group', 'row', 'col'), may hold values from -6 to 6
- counts: int32 [16, 4, 2, 16, 4], P('group', 'row', 'col'), may hold values from 0 to 8, as said below
- tile_rows: int32 [16, 4, 2, 16, 4, 8], P('group', 'row', 'col'), may hold values from 0 to 39, as said below
- tile_cols: int32 [16, 4, 2, 16, 4, 8], P('group', 'row', 'col'), may hold values from 0 to 1
Outputs:
- factored: float32 [16, 20480, 512], P('group', 'row', 'col')
The draws below stay inside these ranges and needn't reach their ends.
Inputs may be any that keep to these rules, and one draw needn't show every extreme that they name: `counts`: slots at or past the count carry nothing; in every draw some owner of some front has 8 live slots from every source, and some fronts receive 8 // 2 or more from every source. `tile_rows`: row tile within the owner's 40 tiles; for grid row 0 never one of the first 2 tiles. `front_entries`: the leading 2 * 128 rows and columns of every front hold a symmetric-part positive definite block.
All inputs are finite; a program needn't handle non-finite values.
Results may differ from the reference program's by a relative error of at most 0.0017.
Values may be sent and summed in bfloat16 or wider, within the bound.
No kernel may reach another device: no remote copies, remote signals or barrier semaphores. Data moves between devices by JAX's collectives and lax.ppermute only.
A program may use at most 128 MiB of HBM per device.

```python
import jax
import jax.numpy as jnp
from jax import lax

F = 20480
PB = 128
NPANEL = 2
CT_DEV = 2
CAP = 8
FRONTS = 16
GRID_ROWS = 4
GRID_COLS = 2
RT_DEV = 40
W = 512


def draw_front_entries(key, part):
    key = jax.random.fold_in(key, 11)
    leading = NPANEL * PB
    row_index = jnp.arange(F, dtype=jnp.int32)[:, None]
    col_index = jnp.arange(W, dtype=jnp.int32)[None, :]
    in_leading = (row_index < leading) & (col_index < leading)
    on_diagonal = (row_index == col_index) & in_leading
    column_scale = jnp.where(col_index < leading, 4.0, 1.0)

    def one_front(front_number):
        front_key = jax.random.fold_in(key, front_number)
        key_base, key_lead, key_diag, key_coupling = jax.random.split(front_key, 4)
        key_size, key_sign = jax.random.split(key_coupling)
        base_draw = jnp.clip(jax.random.normal(key_base, (F, W), jnp.float32), -6.0, 6.0)
        magnitude = jax.random.uniform(key_size, (F,), jnp.float32, 1.0, 3.0)
        signs = jnp.where(jax.random.bernoulli(key_sign, 0.5, (F,)), 1.0, -1.0)
        coupling = magnitude * signs
        outer = coupling[:, None] * coupling[None, :W]
        lead_draw = jax.random.uniform(key_lead, (F, W), jnp.float32, -1.0, 1.0) + outer
        diag_draw = jax.random.uniform(key_diag, (1, W), jnp.float32, leading + 32.0, 2.0 * leading + 32.0)
        values = jnp.where(in_leading, lead_draw + jnp.where(on_diagonal, diag_draw, 0.0), base_draw * column_scale)
        return values.astype(jnp.bfloat16)
    return lax.map(one_front, jnp.arange(FRONTS, dtype=jnp.int32))


def draw_counts(key, part):
    key = jax.random.fold_in(key, 12)
    key_base, key_order, key_high, key_front, key_row, key_col = jax.random.split(key, 6)
    shape = (FRONTS, GRID_ROWS, GRID_COLS, FRONTS, GRID_ROWS)
    base_draw = jax.random.randint(key_base, shape, 0, CAP + 1)
    order = jax.random.permutation(key_order, FRONTS)
    heavy = order < max(1, FRONTS // 4)
    high_draw = jax.random.randint(key_high, shape, CAP // 2, CAP + 1)
    mixed = jnp.where(heavy[:, None, None, None, None], high_draw, base_draw)
    pick_front = jax.random.randint(key_front, (), 0, FRONTS)
    pick_row = jax.random.randint(key_row, (), 0, GRID_ROWS)
    pick_col = jax.random.randint(key_col, (), 0, GRID_COLS)
    full = (lax.broadcasted_iota(jnp.int32, shape, 0) == pick_front) & (lax.broadcasted_iota(jnp.int32, shape, 1) == pick_row) & (lax.broadcasted_iota(jnp.int32, shape, 2) == pick_col)
    return jnp.where(full, CAP, mixed).astype(jnp.int32)


def draw_tile_rows(key, part):
    key = jax.random.fold_in(key, 13)
    shape = (FRONTS, GRID_ROWS, GRID_COLS, FRONTS, GRID_ROWS, CAP)
    lowest = jnp.where(lax.broadcasted_iota(jnp.int32, shape, 1) == 0, NPANEL, 0)
    return jax.random.randint(key, shape, lowest, RT_DEV).astype(jnp.int32)


def with_ends(array, stream_key, low, high):
    dims = array.shape
    index_at = [jax.random.randint(jax.random.fold_in(stream_key, axis), (), 0, dims[axis]) for axis in range(len(dims))]
    array = array.at[tuple(index_at)].set(low)
    longest = dims.index(max(dims))
    index_at[longest] = (index_at[longest] + 1) % dims[longest]
    return array.at[tuple(index_at)].set(high)


def block_scale(rng, shape, pieces, low, largest):
    factor_of, own = 1.0, jax.random.fold_in(rng, 6)
    for dim, parts in pieces:
        draws = jnp.exp(jax.random.uniform(jax.random.fold_in(own, dim), (parts,), jnp.float32, low / len(pieces), largest / len(pieces)))
        factor_of = factor_of * jnp.repeat(draws, shape[dim] // parts).reshape([-1 if axis == dim else 1 for axis in range(len(shape))])
    return factor_of


def scatter_about(stream_key, extent, spread, bound, cuts=(), kind=jnp.bfloat16):
    entries = jax.random.normal(stream_key, extent, jnp.float32) * spread
    if len(cuts) > 0:
        entries = block_scale(stream_key, extent, cuts, -0.22, 0.18) * entries
    return jnp.clip(entries, min=-bound, max=bound).astype(kind)


def setup_inputs(seed: int = 0) -> dict:
    splits = jax.random.split(jax.random.key(seed), 6)
    return {
        "front_entries": draw_front_entries(jax.random.fold_in(splits[5], 71), 0),
        "contrib": scatter_about(splits[1], (FRONTS, GRID_ROWS, GRID_COLS, FRONTS, GRID_ROWS, CAP, PB, PB), 1.0, 6.0, ((0, 16), (1, 4), (2, 2))),
        "counts": draw_counts(jax.random.fold_in(splits[5], 71), 0),
        "tile_rows": draw_tile_rows(jax.random.fold_in(splits[5], 71), 0),
        "tile_cols": with_ends(jax.random.randint(splits[4], (FRONTS, GRID_ROWS, GRID_COLS, FRONTS, GRID_ROWS, CAP), 0, CT_DEV), jax.random.fold_in(splits[4], 1), 0, CT_DEV - 1).astype(jnp.int32),
    }


def assemble_front(front_number, front_entries, contrib, counts, tile_rows, tile_cols):
    matrix = front_entries[front_number].astype(jnp.float32)
    incoming = jnp.transpose(contrib[:, :, :, front_number], (3, 2, 0, 1, 4, 5, 6))
    live_slots = jnp.arange(CAP, dtype=jnp.int32) < counts[front_number][..., None]
    row_tiles = jnp.arange(GRID_ROWS, dtype=jnp.int32)[:, None, None, None, None] * RT_DEV + tile_rows[front_number]
    col_tiles = jnp.arange(GRID_COLS, dtype=jnp.int32)[None, :, None, None, None] * CT_DEV + tile_cols[front_number]
    values = jnp.where(live_slots[..., None, None], incoming.astype(jnp.float32), 0.0)
    tiled = matrix.reshape(F // PB, PB, W // PB, PB).transpose(0, 2, 1, 3)
    tiled = tiled.at[row_tiles.reshape(-1), col_tiles.reshape(-1)].add(values.reshape(-1, PB, PB))
    return tiled.transpose(0, 2, 1, 3).reshape(F, W)

def factor_panels(matrix):
    row_index = jnp.arange(F, dtype=jnp.int32)[:, None]
    col_index = jnp.arange(W, dtype=jnp.int32)[None, :]
    for panel_index in range(NPANEL):
        start_col = panel_index * PB
        stop_col = start_col + PB
        panel_cols = matrix[:, start_col:stop_col]
        factor = jnp.linalg.cholesky(panel_cols[start_col:stop_col])
        solved = jax.scipy.linalg.solve_triangular(factor, panel_cols.T, lower=True).T
        lpanel = solved.at[start_col:stop_col].set(factor)
        lpanel = jnp.where(row_index < start_col, 0.0, lpanel)
        panel_half = lpanel.astype(jnp.bfloat16)
        update = jnp.dot(panel_half.astype(jnp.float32), panel_half[:W].T.astype(jnp.float32), preferred_element_type=jnp.float32)
        matrix = jnp.where(col_index >= stop_col, matrix - update, matrix)
        matrix = matrix.at[:, start_col:stop_col].set(lpanel)
    return matrix

def reference(front_entries, contrib, counts, tile_rows, tile_cols):

    def one_front(front_number):
        matrix = assemble_front(front_number, front_entries, contrib, counts, tile_rows, tile_cols)
        return factor_panels(matrix)
    return lax.map(one_front, jnp.arange(FRONTS, dtype=jnp.int32))
```

```python
import functools

import jax
import jax.numpy as jnp
from jax import lax
from jax.experimental import pallas as pl
from jax.experimental.pallas import tpu as pltpu
from jax.sharding import PartitionSpec as P

PB = 128
CHUNKS = (32, 48, 32, 16)
CHAINS = 4
EXACT = lax.Precision.HIGHEST
VMEM = pl.BlockSpec(memory_space=pltpu.VMEM)


def dot_t(a, b):
    return lax.dot_general(a, b, (((1,), (1,)), ((), ())), preferred_element_type=jnp.float32)


def assemble_kernel(
    rows, tiles, block, target, place, x_ref, e_ref, t1_ref, t2_ref, l21_ref, l11_ref, l22_ref,
    f_ref, h_ref, *acc
):
    step = pl.program_id(0)

    @pl.when(step == 0)
    def _():
        for a in acc:
            a[...] = jnp.zeros_like(a)

    def add(i, carry):
        for j, a in enumerate(acc):
            slot = i * CHAINS + j
            where = pl.ds(pl.multiple_of(target[step * block + slot] * rows, rows), rows)
            a[where, :] += x_ref[slot].astype(jnp.float32)
        return carry

    lax.fori_loop(0, block // CHAINS, add, 0, unroll=4)

    @pl.when(step == pl.num_programs(0) - 1)
    def _():
        batch = 8
        span = batch * rows
        for g in range(tiles // batch):
            parts = []
            for c in range(2):
                here = slice((c * tiles + g * batch) * rows, (c * tiles + g * batch) * rows + span)
                total = acc[0][here, :]
                for a in acc[1:]:
                    total += a[here, :]
                entries = e_ref[g * batch : (g + 1) * batch, :, c * PB : (c + 1) * PB]
                parts.append(total + entries.astype(jnp.float32).reshape(span, PB))
            left, right = parts
            out = slice(g * batch, (g + 1) * batch)

            @pl.when(place[1] == 1)
            def _():
                f_ref[out, :, :PB] = left.reshape(batch, rows, PB)
                f_ref[out, :, PB:] = right.reshape(batch, rows, PB)

            @pl.when(place[1] == 0)
            def _():
                x1 = jnp.dot(left, t1_ref[...], precision=EXACT, preferred_element_type=jnp.float32)
                if g == 0:
                    top = jnp.concatenate([l11_ref[...], x1[rows:]], axis=0)
                    x1 = jnp.where(place[0] == 0, top, x1)
                h1 = x1.astype(jnp.bfloat16)
                right2 = right - dot_t(h1, l21_ref[...])
                x2 = jnp.dot(right2, t2_ref[...], precision=EXACT, preferred_element_type=jnp.float32)
                if g == 0:
                    top = jnp.concatenate([jnp.zeros((rows, PB), jnp.float32), l22_ref[...], x2[2 * rows :]], axis=0)
                    x2 = jnp.where(place[0] == 0, top, x2)
                f_ref[out, :, :PB] = x1.reshape(batch, rows, PB)
                f_ref[out, :, PB:] = x2.reshape(batch, rows, PB)
                h_ref[g * span : (g + 1) * span, :PB] = h1
                h_ref[g * span : (g + 1) * span, PB:] = x2.astype(jnp.bfloat16)


def assemble(target, place, received, entries, t1, t2, l21, l11, l22):
    slots, rows, _ = received.shape
    tiles = entries.shape[0]
    block = 64
    whole = lambda shape: pl.BlockSpec(shape, lambda i, *_: (0,) * len(shape))
    return pl.pallas_call(
        functools.partial(assemble_kernel, rows, tiles, block),
        grid_spec=pltpu.PrefetchScalarGridSpec(
            num_scalar_prefetch=2,
            grid=(slots // block,),
            in_specs=[
                pl.BlockSpec((block, rows, PB), lambda i, *_: (i, 0, 0)),
                whole(entries.shape),
                whole((PB, PB)),
                whole((PB, PB)),
                whole((PB, PB)),
                whole((rows, PB)),
                whole((rows, PB)),
            ],
            out_specs=[whole((tiles, rows, 2 * PB)), whole((tiles * rows, 2 * PB))],
            scratch_shapes=[pltpu.VMEM(((2 * tiles + 1) * rows, PB), jnp.float32)] * CHAINS,
        ),
        out_shape=[
            jax.ShapeDtypeStruct((tiles, rows, 2 * PB), jnp.float32),
            jax.ShapeDtypeStruct((tiles * rows, 2 * PB), jnp.bfloat16),
        ],
        compiler_params=pltpu.CompilerParams(
            dimension_semantics=("arbitrary",), vmem_limit_bytes=40 * 1024 * 1024
        ),
        cost_estimate=pl.CostEstimate(
            flops=slots * rows * PB * 40, bytes_accessed=slots * rows * PB * 2, transcendentals=0
        ),
        name="assemble",
    )(target, place, received, entries, t1, t2, l21, l11, l22)


def update_kernel(chunks, place, *refs):
    n = len(chunks)
    fronts, halves, p_ref, out_ref = refs[:n], refs[n : 2 * n], refs[2 * n], refs[2 * n + 1]
    start = 0
    for rows, f_ref, h_ref in zip(chunks, fronts, halves):
        here = slice(start, start + rows)

        @pl.when(place[1] == 0)
        def _():
            out_ref[:, here, :] = f_ref[...]

        @pl.when(place[1] == 1)
        def _():
            change = dot_t(h_ref[...], p_ref[...])
            out_ref[:, here, :] = f_ref[...] - change.reshape(f_ref.shape)

        start += rows


def update(place, fronts, halves, columns):
    tiles = fronts[0].shape[0]
    batch = 8
    chunks = tuple(f.shape[1] for f in fronts)
    return pl.pallas_call(
        functools.partial(update_kernel, chunks),
        grid_spec=pltpu.PrefetchScalarGridSpec(
            num_scalar_prefetch=1,
            grid=(tiles // batch,),
            in_specs=[pl.BlockSpec((batch, r, 2 * PB), lambda i, *_: (i, 0, 0)) for r in chunks]
            + [pl.BlockSpec((batch * r, 2 * PB), lambda i, *_: (i, 0)) for r in chunks]
            + [pl.BlockSpec((2 * PB, 2 * PB), lambda i, *_: (0, 0))],
            out_specs=pl.BlockSpec((batch, PB, 2 * PB), lambda i, *_: (i, 0, 0)),
        ),
        out_shape=jax.ShapeDtypeStruct((tiles, PB, 2 * PB), jnp.float32),
        compiler_params=pltpu.CompilerParams(
            dimension_semantics=("arbitrary",), vmem_limit_bytes=40 * 1024 * 1024
        ),
        name="update",
    )(place, *fronts, *halves, columns)


def from_first(x, axes, targets, own):
    total = own
    for t in targets:
        total = total + lax.ppermute(x, axes, [(0, t)])
    return total


def after(x, other):
    return lax.optimization_barrier((x, other))[0]


def inverse_t(factor):
    eye = jnp.eye(PB, dtype=jnp.float32)
    return jax.scipy.linalg.solve_triangular(factor, eye, lower=True).T


def local(front_entries, contrib, counts, tile_rows, tile_cols):
    entries = front_entries[0]
    row, col = lax.axis_index("row"), lax.axis_index("col")
    place = jnp.stack([row, col]).astype(jnp.int32)
    tiles = entries.shape[0] // PB
    owners = contrib.shape[3] * contrib.shape[4]
    slots = contrib.shape[5]
    outgoing = contrib.reshape(owners, slots, PB, PB)
    live = jnp.arange(slots, dtype=jnp.int32)[None, :] < counts.reshape(owners)[:, None]
    target = tile_cols.reshape(owners, slots) * tiles + tile_rows.reshape(owners, slots)
    target = jnp.where(live, target, 2 * tiles).reshape(owners * slots)

    lead = entries[: 2 * PB]
    lead = from_first(
        lead, "row", (1, 2, 3), jnp.where(row == 0, lead, jnp.zeros_like(lead))
    ).astype(jnp.float32)
    l11 = jnp.linalg.cholesky(lead[:PB, :PB])
    t1 = inverse_t(l11)
    l21 = jnp.dot(lead[PB:, :PB], t1, precision=EXACT).astype(jnp.bfloat16)
    rest = lead[PB:, PB:] - dot_t(l21, l21)
    l22 = jnp.linalg.cholesky(rest)
    t2 = inverse_t(l22)

    shaped = entries.reshape(tiles, PB, 2 * PB)
    fronts, halves, columns = [], [], []
    received, starts = [], []
    start = 0
    for k, rows in enumerate(CHUNKS):
        stop = start + rows
        starts.append(start)
        source = outgoing
        if k >= 1:
            source = after(source, received[k - 2] if k >= 2 else piece)
        piece = source[:, :, start:stop]
        if k >= 1:
            piece = after(piece, received[k - 1])
        if k >= 2:
            piece = after(piece, halves[k - 2])
        received.append(
            lax.all_to_all(
                piece, ("group", "row"), split_axis=0, concat_axis=0, tiled=True
            ).reshape(owners * slots, rows, PB)
        )
        f, h = assemble(
            target, place, received[k], shaped[:, start:stop], t1, t2, l21, l11[start:stop], l22[start:stop]
        )
        fronts.append(f)
        halves.append(lax.ppermute(h, "col", [(0, 1)]))
        columns.append(h[2 * rows : 4 * rows].reshape(2, rows, 2 * PB))
        start = stop
    last = len(CHUNKS) - 1
    parts = []
    for which in (range(last), (last,)):
        mine = [halves[k][2 * CHUNKS[k] : 4 * CHUNKS[k]].reshape(2, CHUNKS[k], 2 * PB) for k in which]
        mine = jnp.concatenate(mine, axis=1)
        sent = jnp.concatenate([columns[k] for k in which], axis=1)
        parts.append(
            from_first(sent, ("row", "col"), (3, 5, 7), jnp.where(row == 0, mine, jnp.zeros_like(mine)))
        )
    columns = jnp.concatenate(parts, axis=1).reshape(2 * PB, 2 * PB)
    return update(place, fronts, halves, columns).reshape(front_entries.shape)


def solution(mesh):
    placed = (
        P("group", "row", "col"),
        P("group", "row", "col", None, None, None, None, None),
        P("group", "row", "col", None, None),
        P("group", "row", "col", None, None, None),
        P("group", "row", "col", None, None, None),
    )
    return jax.shard_map(
        local, mesh=mesh, in_specs=placed, out_specs=P("group", "row", "col"), check_vma=False
    )
```

```python
import functools

import jax
import jax.numpy as jnp
from jax import lax
from jax.experimental import pallas as pl
from jax.experimental.pallas import tpu as pltpu
from jax.sharding import PartitionSpec as P

PB = 128
CHUNKS = (48, 80)
PIECES = ((0, 0, 16), (0, 16, 32), (1, 0, 48), (1, 48, 32))
CHAINS = 4
DEPTH = 4
BLOCK = 64
EXACT = lax.Precision.HIGHEST
VMEM = pl.BlockSpec(memory_space=pltpu.VMEM)


def dot_t(a, b):
    return lax.dot_general(a, b, (((1,), (1,)), ((), ())), preferred_element_type=jnp.float32)


def assemble_kernel(
    rows, offset, start, target, place, x_hbm, e_hbm, t1_ref, t2_ref, l21_ref, l11_ref, l22_ref, *refs
):
    f_hbm, h_hbm, x_ref, e_ref, f_ref, h_ref, x_sem, e_sem, f_sem, h_sem = refs[-CHAINS - 10 : -CHAINS]
    acc = refs[-CHAINS:]
    slots, tiles = x_ref.shape[0], e_ref.shape[0]
    here = slice(start, start + rows)

    def bring(b):
        part = pl.ds(b * BLOCK, BLOCK)
        return pltpu.make_async_copy(
            x_hbm.at[part, pl.ds(offset, rows), :], x_ref.at[part], x_sem.at[b]
        )

    for b in range(slots // BLOCK):
        bring(b).start()
    entries = pltpu.make_async_copy(e_hbm.at[:, pl.ds(start, rows), :], e_ref, e_sem)
    entries.start()
    for a in acc:
        a[...] = jnp.zeros_like(a)
    group = CHAINS * DEPTH
    for b in range(slots // BLOCK):
        bring(b).wait()

        def add(i, carry):
            base = b * BLOCK + i * group
            spot = [pl.multiple_of(target[base + k] * rows, rows) for k in range(group)]
            for d in range(DEPTH):
                values = []
                for k, a in enumerate(acc):
                    where = pl.ds(spot[d * CHAINS + k], rows)
                    tile = x_ref[base + d * CHAINS + k].astype(jnp.float32)
                    values.append((where, a[where, :] + tile))
                for a, (where, value) in zip(acc, values):
                    a[where, :] = value
            return carry

        lax.fori_loop(0, BLOCK // group, add, 0)
    entries.wait()

    batch = 8
    span = batch * rows
    copies = []
    for g in range(tiles // batch):
        out = slice(g * batch, (g + 1) * batch)
        flat = slice(g * span, (g + 1) * span)
        parts = []
        for c in range(2):
            lines = slice((c * tiles + g * batch) * rows, (c * tiles + g * batch) * rows + span)
            total = e_ref[out, :, c * PB : (c + 1) * PB].astype(jnp.float32).reshape(span, PB)
            for a in acc:
                total += a[lines, :]
            parts.append(total)
        left, right = parts

        @pl.when(place[1] == 1)
        def _():
            f_ref[out, :, :PB] = left.reshape(batch, rows, PB)
            f_ref[out, :, PB:] = right.reshape(batch, rows, PB)

        @pl.when(place[1] == 0)
        def _():
            x1 = jnp.dot(left, t1_ref[...], precision=EXACT, preferred_element_type=jnp.float32)
            if g == 0:
                top = jnp.concatenate([l11_ref[here, :], x1[rows:]], axis=0)
                x1 = jnp.where(place[0] == 0, top, x1)
            h1 = x1.astype(jnp.bfloat16)
            right2 = right - dot_t(h1, l21_ref[...])
            x2 = jnp.dot(right2, t2_ref[...], precision=EXACT, preferred_element_type=jnp.float32)
            if g == 0:
                top = [jnp.zeros((rows, PB), jnp.float32), l22_ref[here, :], x2[2 * rows :]]
                x2 = jnp.where(place[0] == 0, jnp.concatenate(top, axis=0), x2)
            h_ref[flat, :PB] = h1
            h_ref[flat, PB:] = x2.astype(jnp.bfloat16)
            f_ref[out, :, :PB] = x1.reshape(batch, rows, PB)
            f_ref[out, :, PB:] = x2.reshape(batch, rows, PB)

        copies.append(pltpu.make_async_copy(h_ref.at[flat], h_hbm.at[flat], h_sem.at[g]))
        copies.append(pltpu.make_async_copy(f_ref.at[out], f_hbm.at[out, pl.ds(start, rows), :], f_sem.at[g]))
        for copy in copies[-2:]:
            copy.start()
    for copy in copies:
        copy.wait()


def assemble(target, place, received, offset, entries, start, rows, t1, t2, l21, l11, l22, base):
    slots = received.shape[0]
    tiles = entries.shape[0]
    anywhere = pl.BlockSpec(memory_space=pl.ANY)
    square = pl.BlockSpec((PB, PB), lambda i, *_: (0, 0))
    extra = [] if base is None else [base]
    front = jax.ShapeDtypeStruct((tiles, PB, 2 * PB), jnp.float32)
    half = jax.ShapeDtypeStruct((tiles * rows, 2 * PB), jnp.bfloat16)
    return pl.pallas_call(
        functools.partial(assemble_kernel, rows, offset, start),
        grid_spec=pltpu.PrefetchScalarGridSpec(
            num_scalar_prefetch=2,
            grid=(1,),
            in_specs=[anywhere, anywhere] + [square] * 5 + [anywhere] * len(extra),
            out_specs=[anywhere, anywhere],
            scratch_shapes=[
                pltpu.VMEM((slots, rows, PB), jnp.bfloat16),
                pltpu.VMEM((tiles, rows, 2 * PB), jnp.bfloat16),
                pltpu.VMEM((tiles, rows, 2 * PB), front.dtype),
                pltpu.VMEM(half.shape, half.dtype),
                pltpu.SemaphoreType.DMA((slots // BLOCK,)),
                pltpu.SemaphoreType.DMA,
                pltpu.SemaphoreType.DMA((tiles // 8,)),
                pltpu.SemaphoreType.DMA((tiles // 8,)),
            ]
            + [pltpu.VMEM(((2 * tiles + 1) * rows, PB), jnp.float32)] * CHAINS,
        ),
        out_shape=[front, half],
        input_output_aliases={9: 0} if extra else {},
        compiler_params=pltpu.CompilerParams(
            dimension_semantics=("arbitrary",), vmem_limit_bytes=48 * 1024 * 1024
        ),
        cost_estimate=pl.CostEstimate(
            flops=slots * rows * PB * 40, bytes_accessed=slots * rows * PB * 2, transcendentals=0
        ),
        name="assemble",
    )(target, place, received, entries, t1, t2, l21, l11, l22, *extra)


def update_kernel(pieces, place, p_hbm, *refs):
    n = len(pieces)
    halves = refs[:n]
    out_hbm, p_ref, f_ref, h_ref, p_sem, f_sem, h_sem, o_sem = refs[n + 1 :]
    tiles, first = f_ref.shape[0], pieces[0][0]
    batch = 8

    @pl.when(place[1] == 1)
    def _():
        columns = pltpu.make_async_copy(p_hbm, p_ref, p_sem)
        columns.start()
        steps = []
        for g in range(tiles // batch):
            out = slice(g * batch, (g + 1) * batch)
            for h_hbm, (start, rows) in zip(halves, pieces):
                k = len(steps)
                at = pl.ds(start, rows)
                local = pl.ds(start - first, rows)
                lines = pl.ds((start - first) * tiles + g * batch * rows, batch * rows)
                near = f_ref.at[out, local, :]
                bring = [
                    pltpu.make_async_copy(out_hbm.at[out, at, :], near, f_sem.at[k]),
                    pltpu.make_async_copy(
                        h_hbm.at[pl.ds(g * batch * rows, batch * rows)], h_ref.at[lines], h_sem.at[k]
                    ),
                ]
                give = pltpu.make_async_copy(near, out_hbm.at[out, at, :], o_sem.at[k])
                for copy in bring:
                    copy.start()
                steps.append((out, local, lines, rows, bring, give))
        columns.wait()
        for out, local, lines, rows, bring, give in steps:
            for copy in bring:
                copy.wait()
            change = dot_t(h_ref[lines, :], p_ref[...])
            f_ref[out, local, :] -= change.reshape(batch, rows, 2 * PB)
            give.start()
        for step in steps:
            step[-1].wait()


def update(place, front, halves, pieces, columns):
    tiles = front.shape[0]
    rows = sum(r for _, r in pieces)
    steps = len(pieces) * (tiles // 8)
    anywhere = pl.BlockSpec(memory_space=pl.ANY)
    return pl.pallas_call(
        functools.partial(update_kernel, pieces),
        grid_spec=pltpu.PrefetchScalarGridSpec(
            num_scalar_prefetch=1,
            grid=(1,),
            in_specs=[anywhere] * (2 + len(pieces)),
            out_specs=anywhere,
            scratch_shapes=[
                pltpu.VMEM(columns.shape, columns.dtype),
                pltpu.VMEM((tiles, rows, 2 * PB), jnp.float32),
                pltpu.VMEM((tiles * rows, 2 * PB), jnp.bfloat16),
                pltpu.SemaphoreType.DMA,
                pltpu.SemaphoreType.DMA((steps,)),
                pltpu.SemaphoreType.DMA((steps,)),
                pltpu.SemaphoreType.DMA((steps,)),
            ],
        ),
        out_shape=jax.ShapeDtypeStruct(front.shape, front.dtype),
        input_output_aliases={2 + len(pieces): 0},
        compiler_params=pltpu.CompilerParams(
            dimension_semantics=("arbitrary",), vmem_limit_bytes=48 * 1024 * 1024
        ),
        cost_estimate=pl.CostEstimate(
            flops=2 * tiles * rows * 4 * PB * PB, bytes_accessed=tiles * rows * PB * 20, transcendentals=0
        ),
        name="update",
    )(place, columns, *halves, front)


def from_first(x, axes, targets, own):
    total = own
    for t in targets:
        total = total + lax.ppermute(x, axes, [(0, t)])
    return total


def after(x, other):
    return lax.optimization_barrier((x, other))[0]


def exchange(x):
    return lax.all_to_all(x, ("group", "row"), split_axis=0, concat_axis=0, tiled=True)


def inverse_t(factor):
    eye = jnp.eye(PB, dtype=jnp.float32)
    return jax.scipy.linalg.solve_triangular(factor, eye, lower=True).T


def local(front_entries, contrib, counts, tile_rows, tile_cols):
    entries = front_entries[0]
    row, col = lax.axis_index("row"), lax.axis_index("col")
    place = jnp.stack([row, col]).astype(jnp.int32)
    tiles = entries.shape[0] // PB
    owners = contrib.shape[3] * contrib.shape[4]
    slots = contrib.shape[5]
    outgoing = contrib.reshape(owners, slots, PB, PB)
    live = jnp.arange(slots, dtype=jnp.int32)[None, :] < counts.reshape(owners)[:, None]
    target = tile_cols.reshape(owners, slots) * tiles + tile_rows.reshape(owners, slots)
    target = jnp.where(live, target, 2 * tiles).reshape(owners * slots)

    lead = entries[: 2 * PB]
    lead = from_first(
        lead, "row", (1, 2, 3), jnp.where(row == 0, lead, jnp.zeros_like(lead))
    ).astype(jnp.float32)
    l11 = jnp.linalg.cholesky(lead[:PB, :PB])
    t1 = inverse_t(l11)
    l21 = jnp.dot(lead[PB:, :PB], t1, precision=EXACT).astype(jnp.bfloat16)
    rest = lead[PB:, PB:] - dot_t(l21, l21)
    l22 = jnp.linalg.cholesky(rest)
    t2 = inverse_t(l22)

    shaped = entries.reshape(tiles, PB, 2 * PB)
    ready = (target, place, t1, t2, l11, l21, l22)
    piece = after(outgoing[:, :, : CHUNKS[0]], lead)
    first = exchange(piece)
    piece = after(outgoing, piece)[:, :, CHUNKS[0] :]
    first, second = lax.optimization_barrier((first, exchange(after(piece, (first, ready)))))
    received = [r.reshape(owners * slots, -1, PB) for r in (first, second)]

    halves, columns, rows_of = [], [], []
    front, start = None, 0
    for chunk, offset, rows in PIECES:
        tiles_in = received[chunk]
        if len(halves) >= 2:
            tiles_in = after(tiles_in, halves[-2])
        front, h = assemble(
            target, place, tiles_in, offset, shaped, start, rows, t1, t2, l21, l11, l22, front
        )
        columns.append(h[2 * rows : 4 * rows].reshape(2, rows, 2 * PB))
        rows_of.append((start, rows))
        start += rows
        if start == PB:
            columns = jnp.concatenate(columns, axis=1).reshape(2 * PB, 2 * PB)
            columns = from_first(columns, ("row", "col"), (1, 3, 5, 7), jnp.zeros_like(columns))
            h = after(h, columns)
        if len(halves) == 1:
            h = after(h, halves[0])
        halves.append(lax.ppermute(h, "col", [(0, 1)]))
    front = update(place, front, halves[:-1], rows_of[:-1], columns)
    front = update(place, front, halves[-1:], rows_of[-1:], columns)
    return front.reshape(front_entries.shape)


def solution(mesh):
    placed = (
        P("group", "row", "col"),
        P("group", "row", "col", None, None, None, None, None),
        P("group", "row", "col", None, None),
        P("group", "row", "col", None, None, None),
        P("group", "row", "col", None, None, None),
    )
    return jax.shard_map(
        local, mesh=mesh, in_specs=placed, out_specs=P("group", "row", "col"), check_vma=False
    )
```

```python
import functools

import jax
import jax.numpy as jnp
from jax import lax
from jax.experimental import pallas as pl
from jax.experimental.pallas import tpu as pltpu
from jax.sharding import PartitionSpec as P

PB = 128
PIECES = (32, 64, 32)
CHAINS = 4
DEPTH = 4
BLOCK = 64
PIVOTS = 4
EXACT = lax.Precision.HIGHEST
VMEM = pl.BlockSpec(memory_space=pltpu.VMEM)


def dot_t(a, b, precision=None):
    return lax.dot_general(
        a, b, (((1,), (1,)), ((), ())), precision=precision, preferred_element_type=jnp.float32
    )


def split(x):
    high = x.astype(jnp.bfloat16)
    return high, (x - high.astype(jnp.float32)).astype(jnp.bfloat16)


def paired(x):
    high, low = split(x)
    return jnp.concatenate([high, low, high], axis=1)


def solve(x, inverse):
    high, low = split(x)
    return dot_t(jnp.concatenate([high, high, low], axis=1), inverse)


def eliminate(block, raw_ref, unit_ref):
    lane = lax.broadcasted_iota(jnp.int32, (8, PB), 1)
    line = lax.broadcasted_iota(jnp.int32, (8, PB), 0)
    n = PB // 8
    m = [block[8 * k : 8 * k + 8] for k in range(n)]
    for first in range(0, PB, PIVOTS):
        b, s = divmod(first, 8)
        cols = {
            k: [jnp.broadcast_to(m[k][:, first + c : first + c + 1], (8, PB)) for c in range(PIVOTS)]
            for k in range(b, n)
        }
        for c in range(PIVOTS):
            j, own = first + c, s + c
            inverse = 1.0 / cols[b][c][own : own + 1]
            here = lane == j
            pivot = jnp.where(here[:1], 1.0, m[b][own : own + 1]) * inverse
            factors = [cols[b][e][own : own + 1] * inverse for e in range(c + 1, PIVOTS)]
            for k in range(b, n):
                col = cols[k][c]
                raw_ref[8 * k : 8 * k + 8, j : j + 1] = col[:, j : j + 1]
                new = jnp.where(here, 0.0, m[k]) - col * pivot
                m[k] = new if k > b else jnp.where(line > own, new, m[k])
                for e in range(c + 1, PIVOTS):
                    new = cols[k][e] - col * factors[e - c - 1]
                    cols[k][e] = new if k > b else jnp.where(line > own, new, cols[k][e])
    for k in range(n):
        unit_ref[8 * k : 8 * k + 8] = m[k]
    line = lax.broadcasted_iota(jnp.int32, (PB, PB), 0)
    lane = lax.broadcasted_iota(jnp.int32, (PB, PB), 1)
    raw = raw_ref[...]
    diagonal = jnp.where(line == lane, raw, 0.0)
    factor = raw / jnp.sqrt(jnp.sum(diagonal, axis=0, keepdims=True))
    unit = jnp.where(line > lane, unit_ref[...], jnp.where(line == lane, 1.0, 0.0))
    inverse = unit / jnp.sqrt(jnp.sum(diagonal, axis=1, keepdims=True))
    return jnp.where(line >= lane, factor, 0.0), inverse


def factor_kernel(lead_ref, l11_ref, i1_ref, l21_ref, l22_ref, i2_ref, raw_ref, unit_ref):
    def symmetric(block):
        return (block + block.T) * 0.5

    lead = lead_ref[...].astype(jnp.float32)
    factor, inverse = eliminate(symmetric(lead[:PB, :PB]), raw_ref, unit_ref)
    l11_ref[...], i1_ref[...] = factor, paired(inverse)
    l21 = dot_t(lead[PB:, :PB], inverse, EXACT).astype(jnp.bfloat16)
    l21_ref[...] = l21
    rest = symmetric(lead[PB:, PB:]) - dot_t(l21, l21)
    l22_ref[...], inverse = eliminate(rest, raw_ref, unit_ref)
    i2_ref[...] = paired(inverse)


def factor_lead(lead):
    square = jax.ShapeDtypeStruct((PB, PB), jnp.float32)
    wide = jax.ShapeDtypeStruct((PB, 3 * PB), jnp.bfloat16)
    return pl.pallas_call(
        factor_kernel,
        out_shape=[square, wide, jax.ShapeDtypeStruct((PB, PB), jnp.bfloat16), square, wide],
        scratch_shapes=[pltpu.VMEM((PB, PB), jnp.float32)] * 2,
        compiler_params=pltpu.CompilerParams(vmem_limit_bytes=16 * 1024 * 1024),
        name="factor",
    )(lead)


def assemble_kernel(
    rows, offset, start, target, place, x_hbm, e_hbm, i1_ref, i2_ref, l21_ref, l11_ref, l22_ref, *refs
):
    f_hbm, h_hbm, x_ref, e_ref, f_ref, h_ref, x_sem, e_sem, f_sem, h_sem = refs[-CHAINS - 10 : -CHAINS]
    acc = refs[-CHAINS:]
    slots, tiles = x_ref.shape[0], e_ref.shape[0]
    here = slice(start, start + rows)

    def bring(b):
        part = pl.ds(b * BLOCK, BLOCK)
        return pltpu.make_async_copy(
            x_hbm.at[part, pl.ds(offset, rows), :], x_ref.at[part], x_sem.at[b]
        )

    for b in range(slots // BLOCK):
        bring(b).start()
    entries = pltpu.make_async_copy(e_hbm.at[:, pl.ds(start, rows), :], e_ref, e_sem)
    entries.start()
    for a in acc:
        a[...] = jnp.zeros_like(a)
    group = CHAINS * DEPTH
    for b in range(slots // BLOCK):
        bring(b).wait()

        def add(i, carry):
            base = b * BLOCK + i * group
            spot = [pl.multiple_of(target[base + k] * rows, rows) for k in range(group)]
            for d in range(DEPTH):
                values = []
                for k, a in enumerate(acc):
                    where = pl.ds(spot[d * CHAINS + k], rows)
                    tile = x_ref[base + d * CHAINS + k].astype(jnp.float32)
                    values.append((where, a[where, :] + tile))
                for a, (where, value) in zip(acc, values):
                    a[where, :] = value
            return carry

        lax.fori_loop(0, BLOCK // group, add, 0)
    entries.wait()

    batch = 8
    span = batch * rows
    copies = []
    for g in range(tiles // batch):
        out = slice(g * batch, (g + 1) * batch)
        flat = slice(g * span, (g + 1) * span)
        parts = []
        for c in range(2):
            lines = slice((c * tiles + g * batch) * rows, (c * tiles + g * batch) * rows + span)
            total = e_ref[out, :, c * PB : (c + 1) * PB].astype(jnp.float32).reshape(span, PB)
            for a in acc:
                total += a[lines, :]
            parts.append(total)
        left, right = parts

        @pl.when(place[1] == 1)
        def _():
            f_ref[out, :, :PB] = left.reshape(batch, rows, PB)
            f_ref[out, :, PB:] = right.reshape(batch, rows, PB)

        @pl.when(place[1] == 0)
        def _():
            x1 = solve(left, i1_ref[...])
            if g == 0:
                top = jnp.concatenate([l11_ref[here, :], x1[rows:]], axis=0)
                x1 = jnp.where(place[0] == 0, top, x1)
            h1 = x1.astype(jnp.bfloat16)
            right2 = right - dot_t(h1, l21_ref[...])
            x2 = solve(right2, i2_ref[...])
            if g == 0:
                top = [jnp.zeros((rows, PB), jnp.float32), l22_ref[here, :], x2[2 * rows :]]
                x2 = jnp.where(place[0] == 0, jnp.concatenate(top, axis=0), x2)
            h_ref[flat, :PB] = h1
            h_ref[flat, PB:] = x2.astype(jnp.bfloat16)
            f_ref[out, :, :PB] = x1.reshape(batch, rows, PB)
            f_ref[out, :, PB:] = x2.reshape(batch, rows, PB)

        copies.append(pltpu.make_async_copy(h_ref.at[flat], h_hbm.at[flat], h_sem.at[g]))
        copies.append(pltpu.make_async_copy(f_ref.at[out], f_hbm.at[out, pl.ds(start, rows), :], f_sem.at[g]))
        for copy in copies[-2:]:
            copy.start()
    for copy in copies:
        copy.wait()


def assemble(target, place, received, offset, entries, start, rows, i1, i2, l21, l11, l22, base):
    slots = received.shape[0]
    tiles = entries.shape[0]
    anywhere = pl.BlockSpec(memory_space=pl.ANY)
    whole = lambda x: pl.BlockSpec(x.shape, lambda i, *_: (0, 0))
    extra = [] if base is None else [base]
    front = jax.ShapeDtypeStruct((tiles, PB, 2 * PB), jnp.float32)
    half = jax.ShapeDtypeStruct((tiles * rows, 2 * PB), jnp.bfloat16)
    return pl.pallas_call(
        functools.partial(assemble_kernel, rows, offset, start),
        grid_spec=pltpu.PrefetchScalarGridSpec(
            num_scalar_prefetch=2,
            grid=(1,),
            in_specs=[anywhere, anywhere] + [whole(x) for x in (i1, i2, l21, l11, l22)] + [anywhere] * len(extra),
            out_specs=[anywhere, anywhere],
            scratch_shapes=[
                pltpu.VMEM((slots, rows, PB), jnp.bfloat16),
                pltpu.VMEM((tiles, rows, 2 * PB), jnp.bfloat16),
                pltpu.VMEM((tiles, rows, 2 * PB), front.dtype),
                pltpu.VMEM(half.shape, half.dtype),
                pltpu.SemaphoreType.DMA((slots // BLOCK,)),
                pltpu.SemaphoreType.DMA,
                pltpu.SemaphoreType.DMA((tiles // 8,)),
                pltpu.SemaphoreType.DMA((tiles // 8,)),
            ]
            + [pltpu.VMEM(((2 * tiles + 1) * rows, PB), jnp.float32)] * CHAINS,
        ),
        out_shape=[front, half],
        input_output_aliases={9: 0} if extra else {},
        compiler_params=pltpu.CompilerParams(
            dimension_semantics=("arbitrary",), vmem_limit_bytes=48 * 1024 * 1024
        ),
        cost_estimate=pl.CostEstimate(
            flops=slots * rows * PB * 40, bytes_accessed=slots * rows * PB * 2, transcendentals=0
        ),
        name="assemble",
    )(target, place, received, entries, i1, i2, l21, l11, l22, *extra)


def update_kernel(pieces, place, p_hbm, *refs):
    n = len(pieces)
    halves = refs[:n]
    out_hbm, p_ref, f_ref, h_ref, p_sem, f_sem, h_sem, o_sem = refs[n + 1 :]
    tiles, first = f_ref.shape[0], pieces[0][0]
    batch = 8

    @pl.when(place[1] == 1)
    def _():
        columns = pltpu.make_async_copy(p_hbm, p_ref, p_sem)
        columns.start()
        steps = []
        for g in range(tiles // batch):
            out = slice(g * batch, (g + 1) * batch)
            for h_hbm, (start, rows) in zip(halves, pieces):
                k = len(steps)
                at = pl.ds(start, rows)
                local = pl.ds(start - first, rows)
                lines = pl.ds((start - first) * tiles + g * batch * rows, batch * rows)
                near = f_ref.at[out, local, :]
                bring = [
                    pltpu.make_async_copy(out_hbm.at[out, at, :], near, f_sem.at[k]),
                    pltpu.make_async_copy(
                        h_hbm.at[pl.ds(g * batch * rows, batch * rows)], h_ref.at[lines], h_sem.at[k]
                    ),
                ]
                give = pltpu.make_async_copy(near, out_hbm.at[out, at, :], o_sem.at[k])
                for copy in bring:
                    copy.start()
                steps.append((out, local, lines, rows, bring, give))
        columns.wait()
        for out, local, lines, rows, bring, give in steps:
            for copy in bring:
                copy.wait()
            change = dot_t(h_ref[lines, :], p_ref[...])
            f_ref[out, local, :] -= change.reshape(batch, rows, 2 * PB)
            give.start()
        for step in steps:
            step[-1].wait()


def update(place, front, halves, pieces, columns):
    tiles = front.shape[0]
    rows = sum(r for _, r in pieces)
    steps = len(pieces) * (tiles // 8)
    anywhere = pl.BlockSpec(memory_space=pl.ANY)
    return pl.pallas_call(
        functools.partial(update_kernel, pieces),
        grid_spec=pltpu.PrefetchScalarGridSpec(
            num_scalar_prefetch=1,
            grid=(1,),
            in_specs=[anywhere] * (2 + len(pieces)),
            out_specs=anywhere,
            scratch_shapes=[
                pltpu.VMEM(columns.shape, columns.dtype),
                pltpu.VMEM((tiles, rows, 2 * PB), jnp.float32),
                pltpu.VMEM((tiles * rows, 2 * PB), jnp.bfloat16),
                pltpu.SemaphoreType.DMA,
                pltpu.SemaphoreType.DMA((steps,)),
                pltpu.SemaphoreType.DMA((steps,)),
                pltpu.SemaphoreType.DMA((steps,)),
            ],
        ),
        out_shape=jax.ShapeDtypeStruct(front.shape, front.dtype),
        input_output_aliases={2 + len(pieces): 0},
        compiler_params=pltpu.CompilerParams(
            dimension_semantics=("arbitrary",), vmem_limit_bytes=48 * 1024 * 1024
        ),
        cost_estimate=pl.CostEstimate(
            flops=2 * tiles * rows * 4 * PB * PB, bytes_accessed=tiles * rows * PB * 20, transcendentals=0
        ),
        name="update",
    )(place, columns, *halves, front)


def from_first(x, axes, targets, own):
    total = own
    for t in targets:
        total = total + lax.ppermute(x, axes, [(0, t)])
    return total


def after(x, other):
    return lax.optimization_barrier((x, other))[0]


def exchange(x):
    return lax.all_to_all(x, ("group", "row"), split_axis=0, concat_axis=0, tiled=True)


def local(front_entries, contrib, counts, tile_rows, tile_cols):
    entries = front_entries[0]
    row, col = lax.axis_index("row"), lax.axis_index("col")
    place = jnp.stack([row, col]).astype(jnp.int32)
    tiles = entries.shape[0] // PB
    owners = contrib.shape[3] * contrib.shape[4]
    slots = contrib.shape[5]
    outgoing = contrib.reshape(owners, slots, PB, PB)
    live = jnp.arange(slots, dtype=jnp.int32)[None, :] < counts.reshape(owners)[:, None]
    target = tile_cols.reshape(owners, slots) * tiles + tile_rows.reshape(owners, slots)
    target = jnp.where(live, target, 2 * tiles).reshape(owners * slots)

    lead = entries[: 2 * PB]
    lead = from_first(
        lead, "row", (1, 2, 3), jnp.where(row == 0, lead, jnp.zeros_like(lead))
    )
    l11, i1, l21, l22, i2 = factor_lead(lead)
    shaped = entries.reshape(tiles, PB, 2 * PB)
    ready = (target, place, i1, i2, l11, l21, l22)
    received = exchange(after(outgoing, ready)).reshape(owners * slots, PB, PB)

    halves, columns, rows_of = [], [], []
    front, start = None, 0
    for rows in PIECES:
        source = after(received, halves[-2]) if len(halves) >= 2 else received
        front, h = assemble(
            target, place, source, start, shaped, start, rows, i1, i2, l21, l11, l22, front
        )
        columns.append(h[2 * rows : 4 * rows].reshape(2, rows, 2 * PB))
        rows_of.append((start, rows))
        start += rows
        if start == PB:
            columns = jnp.concatenate(columns, axis=1).reshape(2 * PB, 2 * PB)
            near = [lax.ppermute(columns, ("row", "col"), [(0, t)]) for t in (1, 5)]
            near = near[0] + near[1]
            h = after(h, near)
            columns = near + lax.ppermute(near, ("row", "col"), [(1, 3), (5, 7)])
        if len(halves) == 1:
            h = after(h, halves[0])
        halves.append(lax.ppermute(h, "col", [(0, 1)]))
    front = update(place, front, halves[:-1], rows_of[:-1], columns)
    front = update(place, front, halves[-1:], rows_of[-1:], columns)
    return front.reshape(front_entries.shape)


def solution(mesh):
    placed = (
        P("group", "row", "col"),
        P("group", "row", "col", None, None, None, None, None),
        P("group", "row", "col", None, None),
        P("group", "row", "col", None, None, None),
        P("group", "row", "col", None, None, None),
    )
    return jax.shard_map(
        local, mesh=mesh, in_specs=placed, out_specs=P("group", "row", "col"), check_vma=False
    )
```

```python
import functools

import jax
import jax.numpy as jnp
from jax import lax
from jax.experimental import pallas as pl
from jax.experimental.pallas import tpu as pltpu
from jax.sharding import PartitionSpec as P

PB = 128
PIECES = (32, 64, 32)
CHAINS = 4
DEPTH = 4
BLOCK = 64
PIVOTS = 4
EXACT = lax.Precision.HIGHEST
VMEM = pl.BlockSpec(memory_space=pltpu.VMEM)


def dot_t(a, b, precision=None):
    return lax.dot_general(
        a, b, (((1,), (1,)), ((), ())), precision=precision, preferred_element_type=jnp.float32
    )


def split(x):
    high = x.astype(jnp.bfloat16)
    return high, (x - high.astype(jnp.float32)).astype(jnp.bfloat16)


def paired(x):
    high, low = split(x)
    return jnp.concatenate([high, low, high], axis=1)


def solve(x, inverse):
    high, low = split(x)
    return dot_t(jnp.concatenate([high, high, low], axis=1), inverse)


def eliminate(block, raw_ref, unit_ref):
    lane = lax.broadcasted_iota(jnp.int32, (8, PB), 1)
    line = lax.broadcasted_iota(jnp.int32, (8, PB), 0)
    n = PB // 8
    m = [block[8 * k : 8 * k + 8] for k in range(n)]
    for first in range(0, PB, PIVOTS):
        b, s = divmod(first, 8)
        cols = {
            k: [jnp.broadcast_to(m[k][:, first + c : first + c + 1], (8, PB)) for c in range(PIVOTS)]
            for k in range(b, n)
        }
        for c in range(PIVOTS):
            j, own = first + c, s + c
            inverse = 1.0 / cols[b][c][own : own + 1]
            here = lane == j
            pivot = jnp.where(here[:1], 1.0, m[b][own : own + 1]) * inverse
            factors = [cols[b][e][own : own + 1] * inverse for e in range(c + 1, PIVOTS)]
            for k in range(b, n):
                col = cols[k][c]
                raw_ref[8 * k : 8 * k + 8, j : j + 1] = col[:, j : j + 1]
                new = jnp.where(here, 0.0, m[k]) - col * pivot
                m[k] = new if k > b else jnp.where(line > own, new, m[k])
                for e in range(c + 1, PIVOTS):
                    new = cols[k][e] - col * factors[e - c - 1]
                    cols[k][e] = new if k > b else jnp.where(line > own, new, cols[k][e])
    for k in range(n):
        unit_ref[8 * k : 8 * k + 8] = m[k]
    line = lax.broadcasted_iota(jnp.int32, (PB, PB), 0)
    lane = lax.broadcasted_iota(jnp.int32, (PB, PB), 1)
    raw = raw_ref[...]
    diagonal = jnp.where(line == lane, raw, 0.0)
    factor = raw / jnp.sqrt(jnp.sum(diagonal, axis=0, keepdims=True))
    unit = jnp.where(line > lane, unit_ref[...], jnp.where(line == lane, 1.0, 0.0))
    inverse = unit / jnp.sqrt(jnp.sum(diagonal, axis=1, keepdims=True))
    return jnp.where(line >= lane, factor, 0.0), inverse


def factor_kernel(lead_ref, l11_ref, i1_ref, l21_ref, l22_ref, i2_ref, raw_ref, unit_ref):
    def symmetric(block):
        return (block + block.T) * 0.5

    lead = lead_ref[...].astype(jnp.float32)
    factor, inverse = eliminate(symmetric(lead[:PB, :PB]), raw_ref, unit_ref)
    l11_ref[...], i1_ref[...] = factor, paired(inverse)
    l21 = dot_t(lead[PB:, :PB], inverse, EXACT).astype(jnp.bfloat16)
    l21_ref[...] = l21
    rest = symmetric(lead[PB:, PB:]) - dot_t(l21, l21)
    l22_ref[...], inverse = eliminate(rest, raw_ref, unit_ref)
    i2_ref[...] = paired(inverse)


def factor_lead(lead):
    square = jax.ShapeDtypeStruct((PB, PB), jnp.float32)
    wide = jax.ShapeDtypeStruct((PB, 3 * PB), jnp.bfloat16)
    return pl.pallas_call(
        factor_kernel,
        out_shape=[square, wide, jax.ShapeDtypeStruct((PB, PB), jnp.bfloat16), square, wide],
        scratch_shapes=[pltpu.VMEM((PB, PB), jnp.float32)] * 2,
        compiler_params=pltpu.CompilerParams(vmem_limit_bytes=16 * 1024 * 1024),
        name="factor",
    )(lead)


def assemble_kernel(
    rows, offset, start, target, place, x_hbm, e_hbm, i1_ref, i2_ref, l21_ref, l11_ref, l22_ref, *refs
):
    f_hbm, h_hbm, x_ref, e_ref, f_ref, h_ref, x_sem, e_sem, f_sem, h_sem = refs[-CHAINS - 10 : -CHAINS]
    acc = refs[-CHAINS:]
    slots, tiles = x_ref.shape[0], e_ref.shape[0]
    here = slice(start, start + rows)

    def bring(b):
        part = pl.ds(b * BLOCK, BLOCK)
        return pltpu.make_async_copy(
            x_hbm.at[part, pl.ds(offset, rows), :], x_ref.at[part], x_sem.at[b]
        )

    for b in range(slots // BLOCK):
        bring(b).start()
    entries = pltpu.make_async_copy(e_hbm.at[:, pl.ds(start, rows), :], e_ref, e_sem)
    entries.start()
    for a in acc:
        a[...] = jnp.zeros_like(a)
    group = CHAINS * DEPTH
    for b in range(slots // BLOCK):
        bring(b).wait()

        def add(i, carry):
            base = b * BLOCK + i * group
            spot = [pl.multiple_of(target[base + k] * rows, rows) for k in range(group)]
            for d in range(DEPTH):
                values = []
                for k, a in enumerate(acc):
                    where = pl.ds(spot[d * CHAINS + k], rows)
                    tile = x_ref[base + d * CHAINS + k].astype(jnp.float32)
                    values.append((where, a[where, :] + tile))
                for a, (where, value) in zip(acc, values):
                    a[where, :] = value
            return carry

        lax.fori_loop(0, BLOCK // group, add, 0)
    entries.wait()

    batch = 8
    span = batch * rows
    copies = []
    for g in range(tiles // batch):
        out = slice(g * batch, (g + 1) * batch)
        flat = slice(g * span, (g + 1) * span)
        parts = []
        for c in range(2):
            lines = slice((c * tiles + g * batch) * rows, (c * tiles + g * batch) * rows + span)
            total = e_ref[out, :, c * PB : (c + 1) * PB].astype(jnp.float32).reshape(span, PB)
            for a in acc:
                total += a[lines, :]
            parts.append(total)
        left, right = parts

        @pl.when(place[1] == 1)
        def _():
            f_ref[out, :, :PB] = left.reshape(batch, rows, PB)
            f_ref[out, :, PB:] = right.reshape(batch, rows, PB)

        @pl.when(place[1] == 0)
        def _():
            x1 = solve(left, i1_ref[...])
            if g == 0:
                top = jnp.concatenate([l11_ref[here, :], x1[rows:]], axis=0)
                x1 = jnp.where(place[0] == 0, top, x1)
            h1 = x1.astype(jnp.bfloat16)
            right2 = right - dot_t(h1, l21_ref[...])
            x2 = solve(right2, i2_ref[...])
            if g == 0:
                top = [jnp.zeros((rows, PB), jnp.float32), l22_ref[here, :], x2[2 * rows :]]
                x2 = jnp.where(place[0] == 0, jnp.concatenate(top, axis=0), x2)
            h_ref[flat, :PB] = h1
            h_ref[flat, PB:] = x2.astype(jnp.bfloat16)
            f_ref[out, :, :PB] = x1.reshape(batch, rows, PB)
            f_ref[out, :, PB:] = x2.reshape(batch, rows, PB)

        copies.append(pltpu.make_async_copy(h_ref.at[flat], h_hbm.at[flat], h_sem.at[g]))
        copies.append(pltpu.make_async_copy(f_ref.at[out], f_hbm.at[out, pl.ds(start, rows), :], f_sem.at[g]))
        for copy in copies[-2:]:
            copy.start()
    for copy in copies:
        copy.wait()


def assemble(target, place, received, offset, entries, start, rows, i1, i2, l21, l11, l22, base):
    slots = received.shape[0]
    tiles = entries.shape[0]
    anywhere = pl.BlockSpec(memory_space=pl.ANY)
    whole = lambda x: pl.BlockSpec(x.shape, lambda i, *_: (0, 0))
    extra = [] if base is None else [base]
    front = jax.ShapeDtypeStruct((tiles, PB, 2 * PB), jnp.float32)
    half = jax.ShapeDtypeStruct((tiles * rows, 2 * PB), jnp.bfloat16)
    return pl.pallas_call(
        functools.partial(assemble_kernel, rows, offset, start),
        grid_spec=pltpu.PrefetchScalarGridSpec(
            num_scalar_prefetch=2,
            grid=(1,),
            in_specs=[anywhere, anywhere] + [whole(x) for x in (i1, i2, l21, l11, l22)] + [anywhere] * len(extra),
            out_specs=[anywhere, anywhere],
            scratch_shapes=[
                pltpu.VMEM((slots, rows, PB), jnp.bfloat16),
                pltpu.VMEM((tiles, rows, 2 * PB), jnp.bfloat16),
                pltpu.VMEM((tiles, rows, 2 * PB), front.dtype),
                pltpu.VMEM(half.shape, half.dtype),
                pltpu.SemaphoreType.DMA((slots // BLOCK,)),
                pltpu.SemaphoreType.DMA,
                pltpu.SemaphoreType.DMA((tiles // 8,)),
                pltpu.SemaphoreType.DMA((tiles // 8,)),
            ]
            + [pltpu.VMEM(((2 * tiles + 1) * rows, PB), jnp.float32)] * CHAINS,
        ),
        out_shape=[front, half],
        input_output_aliases={9: 0} if extra else {},
        compiler_params=pltpu.CompilerParams(
            dimension_semantics=("arbitrary",), vmem_limit_bytes=48 * 1024 * 1024
        ),
        cost_estimate=pl.CostEstimate(
            flops=slots * rows * PB * 40, bytes_accessed=slots * rows * PB * 2, transcendentals=0
        ),
        name="assemble",
    )(target, place, received, entries, i1, i2, l21, l11, l22, *extra)


def update_kernel(pieces, place, p_hbm, *refs):
    n = len(pieces)
    halves = refs[:n]
    out_hbm, p_ref, f_ref, h_ref, p_sem, f_sem, h_sem, o_sem = refs[n + 1 :]
    tiles, first = f_ref.shape[0], pieces[0][0]
    batch = 8

    @pl.when(place[1] == 1)
    def _():
        columns = pltpu.make_async_copy(p_hbm, p_ref, p_sem)
        columns.start()
        steps = []
        for g in range(tiles // batch):
            out = slice(g * batch, (g + 1) * batch)
            for h_hbm, (start, rows) in zip(halves, pieces):
                k = len(steps)
                at = pl.ds(start, rows)
                local = pl.ds(start - first, rows)
                lines = pl.ds((start - first) * tiles + g * batch * rows, batch * rows)
                near = f_ref.at[out, local, :]
                bring = [
                    pltpu.make_async_copy(out_hbm.at[out, at, :], near, f_sem.at[k]),
                    pltpu.make_async_copy(
                        h_hbm.at[pl.ds(g * batch * rows, batch * rows)], h_ref.at[lines], h_sem.at[k]
                    ),
                ]
                give = pltpu.make_async_copy(near, out_hbm.at[out, at, :], o_sem.at[k])
                for copy in bring:
                    copy.start()
                steps.append((out, local, lines, rows, bring, give))
        columns.wait()
        for out, local, lines, rows, bring, give in steps:
            for copy in bring:
                copy.wait()
            change = dot_t(h_ref[lines, :], p_ref[...])
            f_ref[out, local, :] -= change.reshape(batch, rows, 2 * PB)
            give.start()
        for step in steps:
            step[-1].wait()


def update(place, front, halves, pieces, columns):
    tiles = front.shape[0]
    rows = sum(r for _, r in pieces)
    steps = len(pieces) * (tiles // 8)
    anywhere = pl.BlockSpec(memory_space=pl.ANY)
    return pl.pallas_call(
        functools.partial(update_kernel, pieces),
        grid_spec=pltpu.PrefetchScalarGridSpec(
            num_scalar_prefetch=1,
            grid=(1,),
            in_specs=[anywhere] * (2 + len(pieces)),
            out_specs=anywhere,
            scratch_shapes=[
                pltpu.VMEM(columns.shape, columns.dtype),
                pltpu.VMEM((tiles, rows, 2 * PB), jnp.float32),
                pltpu.VMEM((tiles * rows, 2 * PB), jnp.bfloat16),
                pltpu.SemaphoreType.DMA,
                pltpu.SemaphoreType.DMA((steps,)),
                pltpu.SemaphoreType.DMA((steps,)),
                pltpu.SemaphoreType.DMA((steps,)),
            ],
        ),
        out_shape=jax.ShapeDtypeStruct(front.shape, front.dtype),
        input_output_aliases={2 + len(pieces): 0},
        compiler_params=pltpu.CompilerParams(
            dimension_semantics=("arbitrary",), vmem_limit_bytes=48 * 1024 * 1024
        ),
        cost_estimate=pl.CostEstimate(
            flops=2 * tiles * rows * 4 * PB * PB, bytes_accessed=tiles * rows * PB * 20, transcendentals=0
        ),
        name="update",
    )(place, columns, *halves, front)


def from_first(x, axes, targets, own):
    total = own
    for t in targets:
        total = total + lax.ppermute(x, axes, [(0, t)])
    return total


def after(x, other):
    return lax.optimization_barrier((x, other))[0]


def exchange(x):
    return lax.all_to_all(x, ("group", "row"), split_axis=0, concat_axis=0, tiled=True)


def local(front_entries, contrib, counts, tile_rows, tile_cols):
    entries = front_entries[0]
    row, col = lax.axis_index("row"), lax.axis_index("col")
    place = jnp.stack([row, col]).astype(jnp.int32)
    tiles = entries.shape[0] // PB
    owners = contrib.shape[3] * contrib.shape[4]
    slots = contrib.shape[5]
    outgoing = contrib.reshape(owners, slots, PB, PB)
    live = jnp.arange(slots, dtype=jnp.int32)[None, :] < counts.reshape(owners)[:, None]
    target = tile_cols.reshape(owners, slots) * tiles + tile_rows.reshape(owners, slots)
    target = jnp.where(live, target, 2 * tiles).reshape(owners * slots)

    lead = entries[: 2 * PB]
    lead = from_first(
        lead, "row", (1, 2, 3), jnp.where(row == 0, lead, jnp.zeros_like(lead))
    )
    l11, i1, l21, l22, i2 = factor_lead(lead)
    shaped = entries.reshape(tiles, PB, 2 * PB)
    ready = (target, place, i1, i2, l11, l21, l22)
    received = exchange(after(outgoing, ready)).reshape(owners * slots, PB, PB)

    halves, columns, rows_of = [], [], []
    front, start = None, 0
    for rows in PIECES:
        source = received
        if len(halves) >= 1:
            source = after(source, h)
        if len(halves) >= 2:
            source = after(source, halves[-2])
        front, h = assemble(
            target, place, source, start, shaped, start, rows, i1, i2, l21, l11, l22, front
        )
        columns.append(h[2 * rows : 4 * rows].reshape(2, rows, 2 * PB))
        rows_of.append((start, rows))
        start += rows
        if start == PB:
            columns = jnp.concatenate(columns, axis=1).reshape(2 * PB, 2 * PB)
            near = [lax.ppermute(columns, ("row", "col"), [(0, t)]) for t in (1, 5)]
            near = near[0] + near[1]
            h = after(h, near)
            columns = near + lax.ppermute(near, ("row", "col"), [(1, 3), (5, 7)])
        halves.append(lax.ppermute(h, "col", [(0, 1)]))
    front = update(place, front, halves[:-1], rows_of[:-1], columns)
    front = update(place, front, halves[-1:], rows_of[-1:], columns)
    return front.reshape(front_entries.shape)


def solution(mesh):
    placed = (
        P("group", "row", "col"),
        P("group", "row", "col", None, None, None, None, None),
        P("group", "row", "col", None, None),
        P("group", "row", "col", None, None, None),
        P("group", "row", "col", None, None, None),
    )
    return jax.shard_map(
        local, mesh=mesh, in_specs=placed, out_specs=P("group", "row", "col"), check_vma=False
    )
```

```python
import functools

import jax
import jax.numpy as jnp
from jax import lax
from jax.experimental import pallas as pl
from jax.experimental.pallas import tpu as pltpu
from jax.sharding import PartitionSpec as P

PB = 128
PIECES = (32, 64, 32)
CHAINS = 4
DEPTH = 4
BLOCK = 64
PIVOTS = 8
EXACT = lax.Precision.HIGHEST
VMEM = pl.BlockSpec(memory_space=pltpu.VMEM)


def dot_t(a, b, precision=None):
    return lax.dot_general(
        a, b, (((1,), (1,)), ((), ())), precision=precision, preferred_element_type=jnp.float32
    )


def split(x):
    high = x.astype(jnp.bfloat16)
    return high, (x - high.astype(jnp.float32)).astype(jnp.bfloat16)


def paired(x):
    high, low = split(x)
    return jnp.concatenate([high, low, high], axis=1)


def solve(x, inverse):
    high, low = split(x)
    return dot_t(jnp.concatenate([high, high, low], axis=1), inverse)


def eliminate(block, raw_ref, unit_ref):
    lane = lax.broadcasted_iota(jnp.int32, (8, PB), 1)
    line = lax.broadcasted_iota(jnp.int32, (8, PB), 0)
    n = PB // 8
    m = [block[8 * k : 8 * k + 8] for k in range(n)]
    for first in range(0, PB, PIVOTS):
        b, s = divmod(first, 8)
        cols = {
            k: [jnp.broadcast_to(m[k][:, first + c : first + c + 1], (8, PB)) for c in range(PIVOTS)]
            for k in range(b, n)
        }
        for c in range(PIVOTS):
            j, own = first + c, s + c
            inverse = 1.0 / cols[b][c][own : own + 1]
            here = lane == j
            pivot = jnp.where(here[:1], 1.0, m[b][own : own + 1]) * inverse
            factors = [cols[b][e][own : own + 1] * inverse for e in range(c + 1, PIVOTS)]
            for k in range(b, n):
                col = cols[k][c]
                raw_ref[8 * k : 8 * k + 8, j : j + 1] = col[:, j : j + 1]
                new = jnp.where(here, 0.0, m[k]) - col * pivot
                m[k] = new if k > b else jnp.where(line > own, new, m[k])
                for e in range(c + 1, PIVOTS):
                    new = cols[k][e] - col * factors[e - c - 1]
                    cols[k][e] = new if k > b else jnp.where(line > own, new, cols[k][e])
    for k in range(n):
        unit_ref[8 * k : 8 * k + 8] = m[k]
    line = lax.broadcasted_iota(jnp.int32, (PB, PB), 0)
    lane = lax.broadcasted_iota(jnp.int32, (PB, PB), 1)
    raw = raw_ref[...]
    diagonal = jnp.where(line == lane, raw, 0.0)
    factor = raw / jnp.sqrt(jnp.sum(diagonal, axis=0, keepdims=True))
    unit = jnp.where(line > lane, unit_ref[...], jnp.where(line == lane, 1.0, 0.0))
    inverse = unit / jnp.sqrt(jnp.sum(diagonal, axis=1, keepdims=True))
    return jnp.where(line >= lane, factor, 0.0), inverse


def factor_kernel(lead_ref, l11_ref, i1_ref, l21_ref, l22_ref, i2_ref, raw_ref, unit_ref):
    def symmetric(block):
        return (block + block.T) * 0.5

    lead = lead_ref[...].astype(jnp.float32)
    factor, inverse = eliminate(symmetric(lead[:PB, :PB]), raw_ref, unit_ref)
    l11_ref[...], i1_ref[...] = factor, paired(inverse)
    l21 = dot_t(lead[PB:, :PB], inverse, EXACT).astype(jnp.bfloat16)
    l21_ref[...] = l21
    rest = symmetric(lead[PB:, PB:]) - dot_t(l21, l21)
    l22_ref[...], inverse = eliminate(rest, raw_ref, unit_ref)
    i2_ref[...] = paired(inverse)


def factor_lead(lead):
    square = jax.ShapeDtypeStruct((PB, PB), jnp.float32)
    wide = jax.ShapeDtypeStruct((PB, 3 * PB), jnp.bfloat16)
    return pl.pallas_call(
        factor_kernel,
        out_shape=[square, wide, jax.ShapeDtypeStruct((PB, PB), jnp.bfloat16), square, wide],
        scratch_shapes=[pltpu.VMEM((PB, PB), jnp.float32)] * 2,
        compiler_params=pltpu.CompilerParams(vmem_limit_bytes=16 * 1024 * 1024),
        name="factor",
    )(lead)


def assemble_kernel(
    rows, offset, start, target, place, x_hbm, e_hbm, i1_ref, i2_ref, l21_ref, l11_ref, l22_ref, *refs
):
    f_hbm, h_hbm, x_ref, e_ref, f_ref, h_ref, x_sem, e_sem, f_sem, h_sem = refs[-CHAINS - 10 : -CHAINS]
    acc = refs[-CHAINS:]
    slots, tiles = x_ref.shape[0], e_ref.shape[0]
    here = slice(start, start + rows)

    def bring(b):
        part = pl.ds(b * BLOCK, BLOCK)
        return pltpu.make_async_copy(
            x_hbm.at[part, pl.ds(offset, rows), :], x_ref.at[part], x_sem.at[b]
        )

    for b in range(slots // BLOCK):
        bring(b).start()
    entries = pltpu.make_async_copy(e_hbm.at[:, pl.ds(start, rows), :], e_ref, e_sem)
    entries.start()
    for a in acc:
        a[...] = jnp.zeros_like(a)
    group = CHAINS * DEPTH
    for b in range(slots // BLOCK):
        bring(b).wait()

        def add(i, carry):
            base = b * BLOCK + i * group
            spot = [pl.multiple_of(target[base + k] * rows, rows) for k in range(group)]
            for d in range(DEPTH):
                values = []
                for k, a in enumerate(acc):
                    where = pl.ds(spot[d * CHAINS + k], rows)
                    tile = x_ref[base + d * CHAINS + k].astype(jnp.float32)
                    values.append((where, a[where, :] + tile))
                for a, (where, value) in zip(acc, values):
                    a[where, :] = value
            return carry

        lax.fori_loop(0, BLOCK // group, add, 0)
    entries.wait()

    batch = 8
    span = batch * rows
    copies = []
    for g in range(tiles // batch):
        out = slice(g * batch, (g + 1) * batch)
        flat = slice(g * span, (g + 1) * span)
        parts = []
        for c in range(2):
            lines = slice((c * tiles + g * batch) * rows, (c * tiles + g * batch) * rows + span)
            total = e_ref[out, :, c * PB : (c + 1) * PB].astype(jnp.float32).reshape(span, PB)
            for a in acc:
                total += a[lines, :]
            parts.append(total)
        left, right = parts

        @pl.when(place[1] == 1)
        def _():
            f_ref[out, :, :PB] = left.reshape(batch, rows, PB)
            f_ref[out, :, PB:] = right.reshape(batch, rows, PB)

        @pl.when(place[1] == 0)
        def _():
            x1 = solve(left, i1_ref[...])
            if g == 0:
                top = jnp.concatenate([l11_ref[here, :], x1[rows:]], axis=0)
                x1 = jnp.where(place[0] == 0, top, x1)
            h1 = x1.astype(jnp.bfloat16)
            right2 = right - dot_t(h1, l21_ref[...])
            x2 = solve(right2, i2_ref[...])
            if g == 0:
                top = [jnp.zeros((rows, PB), jnp.float32), l22_ref[here, :], x2[2 * rows :]]
                x2 = jnp.where(place[0] == 0, jnp.concatenate(top, axis=0), x2)
            h_ref[flat, :PB] = h1
            h_ref[flat, PB:] = x2.astype(jnp.bfloat16)
            f_ref[out, :, :PB] = x1.reshape(batch, rows, PB)
            f_ref[out, :, PB:] = x2.reshape(batch, rows, PB)

        copies.append(pltpu.make_async_copy(h_ref.at[flat], h_hbm.at[flat], h_sem.at[g]))
        copies.append(pltpu.make_async_copy(f_ref.at[out], f_hbm.at[out, pl.ds(start, rows), :], f_sem.at[g]))
        for copy in copies[-2:]:
            copy.start()
    for copy in copies:
        copy.wait()


def assemble(target, place, received, offset, entries, start, rows, i1, i2, l21, l11, l22, base):
    slots = received.shape[0]
    tiles = entries.shape[0]
    anywhere = pl.BlockSpec(memory_space=pl.ANY)
    whole = lambda x: pl.BlockSpec(x.shape, lambda i, *_: (0, 0))
    extra = [] if base is None else [base]
    front = jax.ShapeDtypeStruct((tiles, PB, 2 * PB), jnp.float32)
    half = jax.ShapeDtypeStruct((tiles * rows, 2 * PB), jnp.bfloat16)
    return pl.pallas_call(
        functools.partial(assemble_kernel, rows, offset, start),
        grid_spec=pltpu.PrefetchScalarGridSpec(
            num_scalar_prefetch=2,
            grid=(1,),
            in_specs=[anywhere, anywhere] + [whole(x) for x in (i1, i2, l21, l11, l22)] + [anywhere] * len(extra),
            out_specs=[anywhere, anywhere],
            scratch_shapes=[
                pltpu.VMEM((slots, rows, PB), jnp.bfloat16),
                pltpu.VMEM((tiles, rows, 2 * PB), jnp.bfloat16),
                pltpu.VMEM((tiles, rows, 2 * PB), front.dtype),
                pltpu.VMEM(half.shape, half.dtype),
                pltpu.SemaphoreType.DMA((slots // BLOCK,)),
                pltpu.SemaphoreType.DMA,
                pltpu.SemaphoreType.DMA((tiles // 8,)),
                pltpu.SemaphoreType.DMA((tiles // 8,)),
            ]
            + [pltpu.VMEM(((2 * tiles + 1) * rows, PB), jnp.float32)] * CHAINS,
        ),
        out_shape=[front, half],
        input_output_aliases={9: 0} if extra else {},
        compiler_params=pltpu.CompilerParams(
            dimension_semantics=("arbitrary",), vmem_limit_bytes=48 * 1024 * 1024
        ),
        cost_estimate=pl.CostEstimate(
            flops=slots * rows * PB * 40, bytes_accessed=slots * rows * PB * 2, transcendentals=0
        ),
        name="assemble",
    )(target, place, received, entries, i1, i2, l21, l11, l22, *extra)


def update_kernel(pieces, place, p_hbm, *refs):
    n = len(pieces)
    halves = refs[:n]
    out_hbm, p_ref, f_ref, h_ref, p_sem, f_sem, h_sem, o_sem = refs[n + 1 :]
    tiles, first = f_ref.shape[0], pieces[0][0]
    batch = 8

    @pl.when(place[1] == 1)
    def _():
        columns = pltpu.make_async_copy(p_hbm, p_ref, p_sem)
        columns.start()
        steps = []
        for g in range(tiles // batch):
            out = slice(g * batch, (g + 1) * batch)
            for h_hbm, (start, rows) in zip(halves, pieces):
                k = len(steps)
                at = pl.ds(start, rows)
                local = pl.ds(start - first, rows)
                lines = pl.ds((start - first) * tiles + g * batch * rows, batch * rows)
                near = f_ref.at[out, local, :]
                bring = [
                    pltpu.make_async_copy(out_hbm.at[out, at, :], near, f_sem.at[k]),
                    pltpu.make_async_copy(
                        h_hbm.at[pl.ds(g * batch * rows, batch * rows)], h_ref.at[lines], h_sem.at[k]
                    ),
                ]
                give = pltpu.make_async_copy(near, out_hbm.at[out, at, :], o_sem.at[k])
                for copy in bring:
                    copy.start()
                steps.append((out, local, lines, rows, bring, give))
        columns.wait()
        for out, local, lines, rows, bring, give in steps:
            for copy in bring:
                copy.wait()
            change = dot_t(h_ref[lines, :], p_ref[...])
            f_ref[out, local, :] -= change.reshape(batch, rows, 2 * PB)
            give.start()
        for step in steps:
            step[-1].wait()


def update(place, front, halves, pieces, columns):
    tiles = front.shape[0]
    rows = sum(r for _, r in pieces)
    steps = len(pieces) * (tiles // 8)
    anywhere = pl.BlockSpec(memory_space=pl.ANY)
    return pl.pallas_call(
        functools.partial(update_kernel, pieces),
        grid_spec=pltpu.PrefetchScalarGridSpec(
            num_scalar_prefetch=1,
            grid=(1,),
            in_specs=[anywhere] * (2 + len(pieces)),
            out_specs=anywhere,
            scratch_shapes=[
                pltpu.VMEM(columns.shape, columns.dtype),
                pltpu.VMEM((tiles, rows, 2 * PB), jnp.float32),
                pltpu.VMEM((tiles * rows, 2 * PB), jnp.bfloat16),
                pltpu.SemaphoreType.DMA,
                pltpu.SemaphoreType.DMA((steps,)),
                pltpu.SemaphoreType.DMA((steps,)),
                pltpu.SemaphoreType.DMA((steps,)),
            ],
        ),
        out_shape=jax.ShapeDtypeStruct(front.shape, front.dtype),
        input_output_aliases={2 + len(pieces): 0},
        compiler_params=pltpu.CompilerParams(
            dimension_semantics=("arbitrary",), vmem_limit_bytes=48 * 1024 * 1024
        ),
        cost_estimate=pl.CostEstimate(
            flops=2 * tiles * rows * 4 * PB * PB, bytes_accessed=tiles * rows * PB * 20, transcendentals=0
        ),
        name="update",
    )(place, columns, *halves, front)


def from_first(x, axes, targets, own):
    total = own
    for t in targets:
        total = total + lax.ppermute(x, axes, [(0, t)])
    return total


def after(x, other):
    return lax.optimization_barrier((x, other))[0]


def exchange(x):
    return lax.all_to_all(x, ("group", "row"), split_axis=0, concat_axis=0, tiled=True)


def local(front_entries, contrib, counts, tile_rows, tile_cols):
    entries = front_entries[0]
    row, col = lax.axis_index("row"), lax.axis_index("col")
    place = jnp.stack([row, col]).astype(jnp.int32)
    tiles = entries.shape[0] // PB
    owners = contrib.shape[3] * contrib.shape[4]
    slots = contrib.shape[5]
    outgoing = contrib.reshape(owners, slots, PB, PB)
    live = jnp.arange(slots, dtype=jnp.int32)[None, :] < counts.reshape(owners)[:, None]
    target = tile_cols.reshape(owners, slots) * tiles + tile_rows.reshape(owners, slots)
    target = jnp.where(live, target, 2 * tiles).reshape(owners * slots)

    lead = entries[: 2 * PB]
    lead = from_first(
        lead, "row", (1, 2, 3), jnp.where(row == 0, lead, jnp.zeros_like(lead))
    )
    l11, i1, l21, l22, i2 = factor_lead(lead)
    shaped = entries.reshape(tiles, PB, 2 * PB)
    ready = (target, place, i1, i2, l11, l21, l22)
    received = exchange(after(outgoing, ready)).reshape(owners * slots, PB, PB)

    halves, columns, rows_of = [], [], []
    front, start = None, 0
    for rows in PIECES:
        source = received
        if len(halves) >= 1:
            source = after(source, h)
        if len(halves) >= 2:
            source = after(source, halves[-2])
        front, h = assemble(
            target, place, source, start, shaped, start, rows, i1, i2, l21, l11, l22, front
        )
        columns.append(h[2 * rows : 4 * rows].reshape(2, rows, 2 * PB))
        rows_of.append((start, rows))
        start += rows
        if start == PB:
            columns = jnp.concatenate(columns, axis=1).reshape(2 * PB, 2 * PB)
            near = [lax.ppermute(columns, ("row", "col"), [(0, t)]) for t in (1, 5)]
            near = near[0] + near[1]
            h = after(h, near)
            columns = near + lax.ppermute(near, ("row", "col"), [(1, 3), (5, 7)])
        halves.append(lax.ppermute(h, "col", [(0, 1)]))
    front = update(place, front, halves[:-1], rows_of[:-1], columns)
    front = update(place, front, halves[-1:], rows_of[-1:], columns)
    return front.reshape(front_entries.shape)


def solution(mesh):
    placed = (
        P("group", "row", "col"),
        P("group", "row", "col", None, None, None, None, None),
        P("group", "row", "col", None, None),
        P("group", "row", "col", None, None, None),
        P("group", "row", "col", None, None, None),
    )
    return jax.shard_map(
        local, mesh=mesh, in_specs=placed, out_specs=P("group", "row", "col"), check_vma=False
    )
```

```python
import functools

import jax
import jax.numpy as jnp
from jax import lax
from jax.experimental import pallas as pl
from jax.experimental.pallas import tpu as pltpu
from jax.sharding import PartitionSpec as P

PB = 128
PIECES = (32, 64, 32)
CHAINS = 4
DEPTH = 4
BLOCK = 64
PIVOTS = 8
EXACT = lax.Precision.HIGHEST
VMEM = pl.BlockSpec(memory_space=pltpu.VMEM)


def dot_t(a, b, precision=None):
    return lax.dot_general(
        a, b, (((1,), (1,)), ((), ())), precision=precision, preferred_element_type=jnp.float32
    )


def split(x):
    high = x.astype(jnp.bfloat16)
    return high, (x - high.astype(jnp.float32)).astype(jnp.bfloat16)


def paired(x):
    high, low = split(x)
    return jnp.concatenate([high, low, high], axis=1)


def solve(x, inverse):
    high, low = split(x)
    return dot_t(jnp.concatenate([high, high, low], axis=1), inverse)


def eliminate(block, raw_ref, unit_ref):
    lane = lax.broadcasted_iota(jnp.int32, (8, PB), 1)
    line = lax.broadcasted_iota(jnp.int32, (8, PB), 0)
    n = PB // 8
    m = [block[8 * k : 8 * k + 8] for k in range(n)]
    for first in range(0, PB, PIVOTS):
        b, s = divmod(first, 8)
        cols = {
            k: [jnp.broadcast_to(m[k][:, first + c : first + c + 1], (8, PB)) for c in range(PIVOTS)]
            for k in range(b, n)
        }
        for c in range(PIVOTS):
            j, own = first + c, s + c
            inverse = 1.0 / cols[b][c][own : own + 1]
            here = lane == j
            pivot = jnp.where(here[:1], 1.0, m[b][own : own + 1]) * inverse
            factors = [cols[b][e][own : own + 1] * inverse for e in range(c + 1, PIVOTS)]
            for k in range(b, n):
                col = cols[k][c]
                raw_ref[8 * k : 8 * k + 8, j : j + 1] = col[:, j : j + 1]
                new = jnp.where(here, 0.0, m[k]) - col * pivot
                m[k] = new if k > b else jnp.where(line > own, new, m[k])
                for e in range(c + 1, PIVOTS):
                    new = cols[k][e] - col * factors[e - c - 1]
                    cols[k][e] = new if k > b else jnp.where(line > own, new, cols[k][e])
    for k in range(n):
        unit_ref[8 * k : 8 * k + 8] = m[k]
    line = lax.broadcasted_iota(jnp.int32, (PB, PB), 0)
    lane = lax.broadcasted_iota(jnp.int32, (PB, PB), 1)
    raw = raw_ref[...]
    diagonal = jnp.where(line == lane, raw, 0.0)
    factor = raw / jnp.sqrt(jnp.sum(diagonal, axis=0, keepdims=True))
    unit = jnp.where(line > lane, unit_ref[...], jnp.where(line == lane, 1.0, 0.0))
    inverse = unit / jnp.sqrt(jnp.sum(diagonal, axis=1, keepdims=True))
    return jnp.where(line >= lane, factor, 0.0), inverse


def factor_kernel(lead_ref, l11_ref, i1_ref, l21_ref, l22_ref, i2_ref, raw_ref, unit_ref):
    def symmetric(block):
        return (block + block.T) * 0.5

    lead = lead_ref[...].astype(jnp.float32)
    factor, inverse = eliminate(symmetric(lead[:PB, :PB]), raw_ref, unit_ref)
    l11_ref[...], i1_ref[...] = factor, paired(inverse)
    l21 = dot_t(lead[PB:, :PB], inverse, EXACT).astype(jnp.bfloat16)
    l21_ref[...] = l21
    rest = symmetric(lead[PB:, PB:]) - dot_t(l21, l21)
    l22_ref[...], inverse = eliminate(rest, raw_ref, unit_ref)
    i2_ref[...] = paired(inverse)


def factor_lead(lead):
    square = jax.ShapeDtypeStruct((PB, PB), jnp.float32)
    wide = jax.ShapeDtypeStruct((PB, 3 * PB), jnp.bfloat16)
    return pl.pallas_call(
        factor_kernel,
        out_shape=[square, wide, jax.ShapeDtypeStruct((PB, PB), jnp.bfloat16), square, wide],
        scratch_shapes=[pltpu.VMEM((PB, PB), jnp.float32)] * 2,
        compiler_params=pltpu.CompilerParams(vmem_limit_bytes=16 * 1024 * 1024),
        name="factor",
    )(lead)


def assemble_kernel(
    rows, offset, start, target, place, x_hbm, e_hbm, i1_ref, i2_ref, l21_ref, l11_ref, l22_ref, *refs
):
    f_hbm, h_hbm, x_ref, e_ref, f_ref, h_ref, x_sem, e_sem, f_sem, h_sem = refs[-CHAINS - 10 : -CHAINS]
    acc = refs[-CHAINS:]
    slots, tiles = x_ref.shape[0], e_ref.shape[0]
    here = slice(start, start + rows)

    def bring(b):
        part = pl.ds(b * BLOCK, BLOCK)
        return pltpu.make_async_copy(
            x_hbm.at[part, pl.ds(offset, rows), :], x_ref.at[part], x_sem.at[b]
        )

    for b in range(slots // BLOCK):
        bring(b).start()
    entries = pltpu.make_async_copy(e_hbm.at[:, pl.ds(start, rows), :], e_ref, e_sem)
    entries.start()
    for a in acc:
        a[...] = jnp.zeros_like(a)
    group = CHAINS * DEPTH
    for b in range(slots // BLOCK):
        bring(b).wait()

        def add(i, carry):
            base = b * BLOCK + i * group
            spot = [pl.multiple_of(target[base + k] * rows, rows) for k in range(group)]
            for d in range(DEPTH):
                values = []
                for k, a in enumerate(acc):
                    where = pl.ds(spot[d * CHAINS + k], rows)
                    tile = x_ref[base + d * CHAINS + k].astype(jnp.float32)
                    values.append((where, a[where, :] + tile))
                for a, (where, value) in zip(acc, values):
                    a[where, :] = value
            return carry

        lax.fori_loop(0, BLOCK // group, add, 0)
    entries.wait()

    batch = 8
    span = batch * rows
    copies = []
    for g in range(tiles // batch):
        out = slice(g * batch, (g + 1) * batch)
        flat = slice(g * span, (g + 1) * span)
        parts = []
        for c in range(2):
            lines = slice((c * tiles + g * batch) * rows, (c * tiles + g * batch) * rows + span)
            total = e_ref[out, :, c * PB : (c + 1) * PB].astype(jnp.float32).reshape(span, PB)
            for a in acc:
                total += a[lines, :]
            parts.append(total)
        left, right = parts

        @pl.when(place[1] == 1)
        def _():
            f_ref[out, :, :PB] = left.reshape(batch, rows, PB)
            f_ref[out, :, PB:] = right.reshape(batch, rows, PB)

        @pl.when(place[1] == 0)
        def _():
            x1 = solve(left, i1_ref[...])
            if g == 0:
                top = jnp.concatenate([l11_ref[here, :], x1[rows:]], axis=0)
                x1 = jnp.where(place[0] == 0, top, x1)
            h1 = x1.astype(jnp.bfloat16)
            right2 = right - dot_t(h1, l21_ref[...])
            x2 = solve(right2, i2_ref[...])
            if g == 0:
                top = [jnp.zeros((rows, PB), jnp.float32), l22_ref[here, :], x2[2 * rows :]]
                x2 = jnp.where(place[0] == 0, jnp.concatenate(top, axis=0), x2)
            h_ref[flat, :PB] = h1
            h_ref[flat, PB:] = x2.astype(jnp.bfloat16)
            f_ref[out, :, :PB] = x1.reshape(batch, rows, PB)
            f_ref[out, :, PB:] = x2.reshape(batch, rows, PB)

        copies.append(pltpu.make_async_copy(h_ref.at[flat], h_hbm.at[flat], h_sem.at[g]))
        copies.append(pltpu.make_async_copy(f_ref.at[out], f_hbm.at[out, pl.ds(start, rows), :], f_sem.at[g]))
        for copy in copies[-2:]:
            copy.start()
    for copy in copies:
        copy.wait()


def assemble(target, place, received, offset, entries, start, rows, i1, i2, l21, l11, l22, base):
    slots = received.shape[0]
    tiles = entries.shape[0]
    anywhere = pl.BlockSpec(memory_space=pl.ANY)
    whole = lambda x: pl.BlockSpec(x.shape, lambda i, *_: (0, 0))
    extra = [] if base is None else [base]
    front = jax.ShapeDtypeStruct((tiles, PB, 2 * PB), jnp.float32)
    half = jax.ShapeDtypeStruct((tiles * rows, 2 * PB), jnp.bfloat16)
    return pl.pallas_call(
        functools.partial(assemble_kernel, rows, offset, start),
        grid_spec=pltpu.PrefetchScalarGridSpec(
            num_scalar_prefetch=2,
            grid=(1,),
            in_specs=[anywhere, anywhere] + [whole(x) for x in (i1, i2, l21, l11, l22)] + [anywhere] * len(extra),
            out_specs=[anywhere, anywhere],
            scratch_shapes=[
                pltpu.VMEM((slots, rows, PB), jnp.bfloat16),
                pltpu.VMEM((tiles, rows, 2 * PB), jnp.bfloat16),
                pltpu.VMEM((tiles, rows, 2 * PB), front.dtype),
                pltpu.VMEM(half.shape, half.dtype),
                pltpu.SemaphoreType.DMA((slots // BLOCK,)),
                pltpu.SemaphoreType.DMA,
                pltpu.SemaphoreType.DMA((tiles // 8,)),
                pltpu.SemaphoreType.DMA((tiles // 8,)),
            ]
            + [pltpu.VMEM(((2 * tiles + 1) * rows, PB), jnp.float32)] * CHAINS,
        ),
        out_shape=[front, half],
        input_output_aliases={9: 0} if extra else {},
        compiler_params=pltpu.CompilerParams(
            dimension_semantics=("arbitrary",), vmem_limit_bytes=48 * 1024 * 1024
        ),
        cost_estimate=pl.CostEstimate(
            flops=slots * rows * PB * 40, bytes_accessed=slots * rows * PB * 2, transcendentals=0
        ),
        name="assemble",
    )(target, place, received, entries, i1, i2, l21, l11, l22, *extra)


def update_kernel(pieces, place, p_hbm, *refs):
    n = len(pieces)
    halves = refs[:n]
    out_hbm, p_ref, f_ref, h_ref, p_sem, f_sem, h_sem, o_sem = refs[n + 1 :]
    tiles, first = f_ref.shape[0], pieces[0][0]
    batch = 20

    @pl.when(place[1] == 1)
    def _():
        columns = pltpu.make_async_copy(p_hbm, p_ref, p_sem)
        columns.start()
        steps = []
        for g in range(tiles // batch):
            out = slice(g * batch, (g + 1) * batch)
            for h_hbm, (start, rows) in zip(halves, pieces):
                k = len(steps)
                at = pl.ds(start, rows)
                local = pl.ds(start - first, rows)
                lines = pl.ds((start - first) * tiles + g * batch * rows, batch * rows)
                near = f_ref.at[out, local, :]
                bring = [
                    pltpu.make_async_copy(out_hbm.at[out, at, :], near, f_sem.at[k]),
                    pltpu.make_async_copy(
                        h_hbm.at[pl.ds(g * batch * rows, batch * rows)], h_ref.at[lines], h_sem.at[k]
                    ),
                ]
                give = pltpu.make_async_copy(near, out_hbm.at[out, at, :], o_sem.at[k])
                for copy in bring:
                    copy.start()
                steps.append((out, local, lines, rows, bring, give))
        columns.wait()
        for out, local, lines, rows, bring, give in steps:
            for copy in bring:
                copy.wait()
            change = dot_t(h_ref[lines, :], p_ref[...])
            f_ref[out, local, :] -= change.reshape(batch, rows, 2 * PB)
            give.start()
        for step in steps:
            step[-1].wait()


def update(place, front, halves, pieces, columns):
    tiles = front.shape[0]
    rows = sum(r for _, r in pieces)
    steps = len(pieces) * (tiles // 20)
    anywhere = pl.BlockSpec(memory_space=pl.ANY)
    return pl.pallas_call(
        functools.partial(update_kernel, pieces),
        grid_spec=pltpu.PrefetchScalarGridSpec(
            num_scalar_prefetch=1,
            grid=(1,),
            in_specs=[anywhere] * (2 + len(pieces)),
            out_specs=anywhere,
            scratch_shapes=[
                pltpu.VMEM(columns.shape, columns.dtype),
                pltpu.VMEM((tiles, rows, 2 * PB), jnp.float32),
                pltpu.VMEM((tiles * rows, 2 * PB), jnp.bfloat16),
                pltpu.SemaphoreType.DMA,
                pltpu.SemaphoreType.DMA((steps,)),
                pltpu.SemaphoreType.DMA((steps,)),
                pltpu.SemaphoreType.DMA((steps,)),
            ],
        ),
        out_shape=jax.ShapeDtypeStruct(front.shape, front.dtype),
        input_output_aliases={2 + len(pieces): 0},
        compiler_params=pltpu.CompilerParams(
            dimension_semantics=("arbitrary",), vmem_limit_bytes=48 * 1024 * 1024
        ),
        cost_estimate=pl.CostEstimate(
            flops=2 * tiles * rows * 4 * PB * PB, bytes_accessed=tiles * rows * PB * 20, transcendentals=0
        ),
        name="update",
    )(place, columns, *halves, front)


def from_first(x, axes, targets, own):
    total = own
    for t in targets:
        total = total + lax.ppermute(x, axes, [(0, t)])
    return total


def after(x, other):
    return lax.optimization_barrier((x, other))[0]


def exchange(x):
    return lax.all_to_all(x, ("group", "row"), split_axis=0, concat_axis=0, tiled=True)


def local(front_entries, contrib, counts, tile_rows, tile_cols):
    entries = front_entries[0]
    row, col = lax.axis_index("row"), lax.axis_index("col")
    place = jnp.stack([row, col]).astype(jnp.int32)
    tiles = entries.shape[0] // PB
    owners = contrib.shape[3] * contrib.shape[4]
    slots = contrib.shape[5]
    outgoing = contrib.reshape(owners, slots, PB, PB)
    live = jnp.arange(slots, dtype=jnp.int32)[None, :] < counts.reshape(owners)[:, None]
    target = tile_cols.reshape(owners, slots) * tiles + tile_rows.reshape(owners, slots)
    target = jnp.where(live, target, 2 * tiles).reshape(owners * slots)

    lead = entries[: 2 * PB]
    lead = from_first(
        lead, "row", (1, 2, 3), jnp.where(row == 0, lead, jnp.zeros_like(lead))
    )
    l11, i1, l21, l22, i2 = factor_lead(lead)
    shaped = entries.reshape(tiles, PB, 2 * PB)
    ready = (target, place, i1, i2, l11, l21, l22)
    received = exchange(after(outgoing, ready)).reshape(owners * slots, PB, PB)

    halves, columns, rows_of = [], [], []
    front, start = None, 0
    for rows in PIECES:
        source = received
        if len(halves) >= 1:
            source = after(source, h)
        if len(halves) >= 2:
            source = after(source, halves[-2])
        front, h = assemble(
            target, place, source, start, shaped, start, rows, i1, i2, l21, l11, l22, front
        )
        columns.append(h[2 * rows : 4 * rows].reshape(2, rows, 2 * PB))
        rows_of.append((start, rows))
        start += rows
        if start == PB:
            columns = jnp.concatenate(columns, axis=1).reshape(2 * PB, 2 * PB)
            near = [lax.ppermute(columns, ("row", "col"), [(0, t)]) for t in (1, 5)]
            near = near[0] + near[1]
            h = after(h, near)
            columns = near + lax.ppermute(near, ("row", "col"), [(1, 3), (5, 7)])
        halves.append(lax.ppermute(h, "col", [(0, 1)]))
    front = update(place, front, halves[:-1], rows_of[:-1], columns)
    front = update(place, front, halves[-1:], rows_of[-1:], columns)
    return front.reshape(front_entries.shape)


def solution(mesh):
    placed = (
        P("group", "row", "col"),
        P("group", "row", "col", None, None, None, None, None),
        P("group", "row", "col", None, None),
        P("group", "row", "col", None, None, None),
        P("group", "row", "col", None, None, None),
    )
    return jax.shard_map(
        local, mesh=mesh, in_specs=placed, out_specs=P("group", "row", "col"), check_vma=False
    )
```
